32 devices in a mesh: seq: 16 (over z, x, core), head: 2 (over y).
Axes of the slice: x: 2, y: 2, z: 4, core: 2. Of those that a mesh axis runs over, the one named last changes fastest.
Arguments:
- queries: bfloat16 [16384, 3072], P('seq', 'head'), may hold values from -6 to 6
- keys: bfloat16 [16384, 3072], P('seq', 'head'), may hold values from -6 to 6
- values: bfloat16 [16384, 3072], P('seq', 'head'), may hold values from -6 to 6
- tile_pool: int32 [24, 256], P('head'), may hold values from 0 to 127, as said below
- tile_lists: int32 [24, 128, 12], P('head', 'seq'), may hold values from 0 to 15, as said below
- key_slot: int32 [128], replicated, may hold values from 0 to 127, as said below
Outputs:
- attended: bfloat16 [16384, 3072], P(('seq', 'head'))
The draws below stay inside these ranges and needn't reach their ends.
Inputs may be any that keep to these rules, and one draw needn't show every extreme that they name: `tile_pool`: for each index i of seq and each group of 12 heads (heads g * 12 onward), the pool entries of those heads for index i (columns i * 16 onward) name tiles whose slots lie on any one index of seq (slot // 8) at most 12 times, and exactly 12 times on some index. `tile_lists`: the 12 entries of one head and one query tile are distinct. `key_slot`: A permutation of the tiles that keeps tiles 0 to 3 at their own slots.
All inputs are finite; a program needn't handle non-finite values.
Results may differ from the reference program's by a relative error of at most 0.0043.
Values may be sent and summed in bfloat16 or wider, within the bound.
No kernel may reach another device: no remote copies, remote signals or barrier semaphores. Data moves between devices by JAX's collectives and lax.ppermute only.
A program may use at most 128 MiB of HBM per device.

```python
import jax
import jax.numpy as jnp
from jax import lax

HEADS = 24
HD = 128
TILE = 128
TILES_DEV = 8
LIST = 12
POOL = 16
SHARED = 4
HEADS_DEV = 12
NTILES = 128
POOLS = 256
TOKENS = 16384
WIDTH = 3072


def slot_table(key):
    others = jax.random.permutation(jax.random.fold_in(key, 21), NTILES - SHARED) + SHARED
    return jnp.concatenate([jnp.arange(SHARED, dtype=jnp.int32), others.astype(jnp.int32)])


def draw_key_slot(key, part):
    return slot_table(key)


def draw_tile_pool(key, part):
    slots_of = slot_table(key)
    inverse = jnp.argsort(slots_of).astype(jnp.int32)
    seq_count = POOLS // POOL
    groups = HEADS // HEADS_DEV
    demand = HEADS_DEV * POOL
    bound_slots = (demand + seq_count - 1) // seq_count

    def one_block(block_key):
        spread = jax.random.permutation(jax.random.fold_in(block_key, 1), bound_slots * seq_count)
        owners = (spread % seq_count)[:demand].astype(jnp.int32)
        local_tiles = jax.random.randint(jax.random.fold_in(block_key, 2), (demand,), 0, TILES_DEV).astype(jnp.int32)
        return inverse[owners * TILES_DEV + local_tiles].reshape(HEADS_DEV, POOL)
    block_keys = jax.random.split(jax.random.fold_in(key, 31), seq_count * groups)
    blocks = jax.vmap(one_block)(block_keys).reshape(seq_count, groups, HEADS_DEV, POOL)
    return blocks.transpose(1, 2, 0, 3).reshape(HEADS, POOLS).astype(jnp.int32)


def draw_tile_lists(key, part):
    row_keys = jax.random.split(jax.random.fold_in(key, 51), HEADS * NTILES)

    def one_row(row_key):
        return jax.random.permutation(row_key, POOL)[:LIST].astype(jnp.int32)
    return jax.vmap(one_row)(row_keys).reshape(HEADS, NTILES, LIST).astype(jnp.int32)


def draw_keys(key, part):
    total_rows = NTILES * TILE
    sample = jax.random.normal(jax.random.fold_in(key, 5), (total_rows, HEADS * HD), jnp.float32)
    return jnp.clip(sample, -6.0, 6.0).astype(jnp.bfloat16)


def draw_queries(key, part):
    total_rows = NTILES * TILE
    sample = jax.random.normal(jax.random.fold_in(key, 7), (total_rows, HEADS * HD), jnp.float32)
    return jnp.clip(sample, -6.0, 6.0).astype(jnp.bfloat16)


def levels(rng, extent, pieces, low, top_value):
    level = 1.0
    for axis_at, shards_of in pieces:
        heights = jax.random.uniform(jax.random.fold_in(jax.random.fold_in(rng, 6), axis_at), (shards_of,), jnp.float32, low / len(pieces), top_value / len(pieces))
        level = level * jnp.repeat(jnp.exp(heights), extent[axis_at] // shards_of).reshape((-1,) + (1,) * (len(extent) - 1 - axis_at))
    return level


def gaussian(stream_key, dims, deviation, reach, cuts=(), kind=jnp.bfloat16):
    values = jax.random.normal(stream_key, dims, jnp.float32) * deviation
    if len(cuts) > 0:
        values = levels(stream_key, dims, cuts, -0.22, 0.18) * values
    return jnp.clip(values, min=-reach, max=reach).astype(kind)


def setup_inputs(seed: int = 0) -> dict:
    key_list = jax.random.split(jax.random.key(seed), 7)
    queries = draw_queries(jax.random.fold_in(key_list[6], 71), 0)
    keys = draw_keys(jax.random.fold_in(key_list[6], 71), 0)
    values = gaussian(key_list[2], (TOKENS, WIDTH), 1.0, 6.0, ((0, 16), (1, 2)))
    tile_pool = draw_tile_pool(jax.random.fold_in(key_list[6], 71), 0)
    tile_lists = draw_tile_lists(jax.random.fold_in(key_list[6], 71), 0)
    key_slot = draw_key_slot(jax.random.fold_in(key_list[6], 71), 0)
    return dict(queries=queries, keys=keys, values=values, tile_pool=tile_pool, tile_lists=tile_lists, key_slot=key_slot)


def reference(queries, keys, values, tile_pool, tile_lists, key_slot):
    scaling = HD ** -0.5
    query_tiles = queries.reshape(NTILES, TILE, HEADS, HD).transpose(2, 0, 1, 3)
    key_tiles = keys.reshape(NTILES, TILE, HEADS, HD).transpose(2, 0, 1, 3)
    value_tiles = values.reshape(NTILES, TILE, HEADS, HD).transpose(2, 0, 1, 3)
    shared_ids = jnp.arange(SHARED).astype(jnp.int32)
    tile_ids = jnp.arange(NTILES).astype(jnp.int32)

    def one_head(member):
        query_head, key_head, value_head, pool_head, lists_head = member

        def one_tile(query_tile, list_row, tile_id):
            entries = ((tile_id // TILES_DEV) * POOL + list_row).astype(jnp.int32)
            chosen = jnp.concatenate([shared_ids, pool_head[entries].astype(jnp.int32)])
            storage = key_slot[chosen].astype(jnp.int32)
            key_sel = key_head[storage].astype(jnp.float32)
            value_sel = value_head[storage].astype(jnp.float32)
            scores = jnp.einsum("qd,jkd->jqk", query_tile.astype(jnp.float32), key_sel) * scaling
            tile_top = jnp.max(scores, -1)
            weights = jnp.exp(scores - tile_top[..., None])
            row_total = jnp.sum(weights, -1)
            rounded = lax.optimization_barrier(weights.astype(jnp.bfloat16)).astype(jnp.float32)
            numerator = jnp.einsum("jqk,jkd->jqd", rounded, value_sel)
            overall = jnp.max(tile_top, 0)
            factor = jnp.exp(tile_top - overall[None, :])
            upper = jnp.sum(factor[..., None] * numerator, 0)
            lower = jnp.sum(factor * row_total, 0)
            return (upper / lower[:, None]).astype(jnp.bfloat16)

        return jax.vmap(one_tile)(query_head, lists_head, tile_ids)

    result = lax.map(one_head, (query_tiles, key_tiles, value_tiles, tile_pool, tile_lists))
    return result.transpose(1, 2, 0, 3).reshape(NTILES * TILE, HEADS * HD)
```

```python
import functools

import jax
import jax.numpy as jnp
from jax import lax
from jax.experimental import pallas as pl
from jax.experimental.pallas import tpu as pltpu
from jax.sharding import PartitionSpec as P

TILE = 128
SHARED = 4
FAR = 1e30
LOG2E = 1.4426950408889634
VMEM_BYTES = 56 * 1024 * 1024


def pack_kernel(head_size, codes_ref, keys_ref, values_ref, out_ref, sem):
    def start(i, _):
        code = codes_ref[i]
        slot = code % 65536
        head = code // 65536
        rows = pl.ds(pl.multiple_of(slot * TILE, TILE), TILE)
        cols = pl.ds(pl.multiple_of(head * head_size, head_size), head_size)
        pltpu.make_async_copy(keys_ref.at[rows, cols], out_ref.at[i, 0], sem).start()
        pltpu.make_async_copy(values_ref.at[rows, cols], out_ref.at[i, 1], sem).start()
        return 0

    lax.fori_loop(0, out_ref.shape[0], start, 0)
    pltpu.make_async_copy(out_ref, out_ref, sem).wait()


def pack(codes, keys, values, head_size):
    count = codes.shape[0]
    return pl.pallas_call(
        functools.partial(pack_kernel, head_size),
        out_shape=jax.ShapeDtypeStruct((count, 2, TILE, head_size), keys.dtype),
        in_specs=[
            pl.BlockSpec(memory_space=pltpu.SMEM),
            pl.BlockSpec(memory_space=pl.ANY),
            pl.BlockSpec(memory_space=pl.ANY),
        ],
        out_specs=pl.BlockSpec(memory_space=pl.ANY),
        scratch_shapes=[pltpu.SemaphoreType.DMA],
        cost_estimate=pl.CostEstimate(
            flops=0, bytes_accessed=4 * count * 2 * TILE * head_size, transcendentals=0
        ),
        name="pack_tiles",
    )(codes, keys, values)


def shared_kernel(scale, block, q_ref, kv_ref, qt_ref, acc_ref, m_ref, l_ref):
    rows = q_ref.shape[0]
    head_size = q_ref.shape[1]
    qt_ref[0] = q_ref[...].T
    k = kv_ref[0, :, 0].reshape(-1, head_size)
    vt = kv_ref[0, :, 1].reshape(-1, head_size).T
    for start in range(0, rows, block):
        cols = slice(start, start + block)
        s = jnp.dot(k, qt_ref[0, :, cols], preferred_element_type=jnp.float32)
        m = jnp.max(s, 0, keepdims=True) * scale
        p = jnp.exp2(s * scale - m)
        m_ref[0, :, cols] = m
        l_ref[0, :, cols] = jnp.sum(p, 0, keepdims=True)
        acc_ref[0, :, cols] = jnp.dot(
            vt, p.astype(jnp.bfloat16), preferred_element_type=jnp.float32
        )


def shared_part(queries, shared, head_count, head_size, scale):
    rows = queries.shape[0]
    state = jax.ShapeDtypeStruct((head_count, 1, rows), jnp.float32)
    stat_spec = pl.BlockSpec((1, 1, rows), lambda h: (h, 0, 0))
    wide_spec = pl.BlockSpec((1, head_size, rows), lambda h: (h, 0, 0))
    return pl.pallas_call(
        functools.partial(shared_kernel, scale, min(256, rows)),
        grid=(head_count,),
        out_shape=(
            jax.ShapeDtypeStruct((head_count, head_size, rows), jnp.bfloat16),
            jax.ShapeDtypeStruct((head_count, head_size, rows), jnp.float32),
            state,
            state,
        ),
        in_specs=[
            pl.BlockSpec((rows, head_size), lambda h: (0, h)),
            pl.BlockSpec((1, SHARED, 2, TILE, head_size), lambda h: (h, 0, 0, 0, 0)),
        ],
        out_specs=(wide_spec, wide_spec, stat_spec, stat_spec),
        compiler_params=pltpu.CompilerParams(vmem_limit_bytes=VMEM_BYTES),
        cost_estimate=pl.CostEstimate(
            flops=4 * head_count * rows * SHARED * TILE * head_size,
            bytes_accessed=16 * head_count * rows * head_size,
            transcendentals=head_count * rows * SHARED * TILE,
        ),
        name="shared_tiles",
    )(queries, shared)


def pool_kernel(
    scale, block, last, where_ref, entry_ref, count_ref,
    qt_ref, tiles_ref, bias_ref, acc_in, m_in, l_in, *rest,
):
    if last:
        out_ref, acc_ref, m_ref, l_ref = rest
    else:
        acc_ref, m_ref, l_ref = rest
    head = pl.program_id(0)
    rows = qt_ref.shape[2]
    acc_ref[...] = acc_in[...]
    m_ref[...] = m_in[...]
    l_ref[...] = l_in[...]

    def one(i, _):
        tile = where_ref[head, i]
        entry = entry_ref[head, i]
        k = tiles_ref[tile, 0]
        vt = tiles_ref[tile, 1].T
        for start in range(0, rows, block):
            cols = slice(start, start + block)
            s = jnp.dot(k, qt_ref[0, :, cols], preferred_element_type=jnp.float32)
            bias = bias_ref[0, pl.ds(entry, 1), cols]
            top = jnp.max(s, 0, keepdims=True) * scale + bias
            m_old = m_ref[0, :, cols]
            m_new = jnp.maximum(m_old, top)
            alpha = jnp.exp2(m_old - m_new)
            p = jnp.exp2(s * scale - (m_new - bias))
            m_ref[0, :, cols] = m_new
            l_ref[0, :, cols] = l_ref[0, :, cols] * alpha + jnp.sum(p, 0, keepdims=True)
            acc_ref[0, :, cols] = acc_ref[0, :, cols] * alpha + jnp.dot(
                vt, p.astype(jnp.bfloat16), preferred_element_type=jnp.float32
            )
        return 0

    lax.fori_loop(0, count_ref[head], one, 0)
    if last:
        for start in range(0, rows, block):
            cols = slice(start, start + block)
            out = (acc_ref[0, :, cols] / l_ref[0, :, cols]).astype(jnp.bfloat16)
            out_ref[cols, :] = out.T


def pool_part(tables, qt, tiles, bias, acc, m, l, scale, last):
    head_count, head_size, rows = qt.shape
    pool_len = bias.shape[1]
    stat_spec = pl.BlockSpec((1, 1, rows), lambda h, *_: (h, 0, 0))
    wide_spec = pl.BlockSpec((1, head_size, rows), lambda h, *_: (h, 0, 0))
    if last:
        out_shape = jax.ShapeDtypeStruct((rows, head_count * head_size), jnp.bfloat16)
        out_specs = pl.BlockSpec((rows, head_size), lambda h, *_: (0, h))
        scratch = [
            pltpu.VMEM((1, head_size, rows), jnp.float32),
            pltpu.VMEM((1, 1, rows), jnp.float32),
            pltpu.VMEM((1, 1, rows), jnp.float32),
        ]
    else:
        out_shape = tuple(jax.ShapeDtypeStruct(a.shape, a.dtype) for a in (acc, m, l))
        out_specs = (wide_spec, stat_spec, stat_spec)
        scratch = []
    work = tiles.shape[0] * rows * TILE
    return pl.pallas_call(
        functools.partial(pool_kernel, scale, min(256, rows), last),
        grid_spec=pltpu.PrefetchScalarGridSpec(
            num_scalar_prefetch=3,
            grid=(head_count,),
            in_specs=[
                wide_spec,
                pl.BlockSpec(tiles.shape, lambda h, *_: (0, 0, 0, 0), pipeline_mode=pl.Buffered(1)),
                pl.BlockSpec((1, pool_len, rows), lambda h, *_: (h, 0, 0)),
                wide_spec,
                stat_spec,
                stat_spec,
            ],
            out_specs=out_specs,
            scratch_shapes=scratch,
        ),
        out_shape=out_shape,
        compiler_params=pltpu.CompilerParams(vmem_limit_bytes=VMEM_BYTES),
        cost_estimate=pl.CostEstimate(
            flops=4 * work * head_size,
            bytes_accessed=10 * head_count * rows * head_size,
            transcendentals=work,
        ),
        name="pool_tiles",
    )(*tables, qt, tiles, bias, acc, m, l)


def spread_shared(pieces, axis):
    count = lax.axis_size(axis)
    me = lax.axis_index(axis)
    step = count // 2
    while step >= 1:
        pairs = [(i, i + step) for i in range(0, count, 2 * step)]
        got = lax.ppermute(pieces[step:], axis, pairs)
        pieces = jnp.where(me % (2 * step) == step, got, pieces[:step])
        step //= 2
    return pieces


def chunk_edges(total):
    if total < 6:
        return [0, total]
    last = max(1, total // 12)
    return [0, (total * 5) // 12, (total * 9) // 12, total - last, total]


def body(queries, keys, values, tile_pool, tile_lists, key_slot):
    seq_count = lax.axis_size("seq")
    me = lax.axis_index("seq")
    head_count, pool_total = tile_pool.shape
    pool_len = pool_total // seq_count
    rows, width = queries.shape
    head_size = width // head_count
    tile_count = rows // TILE
    bound = (head_count * pool_len + seq_count - 1) // seq_count
    scale = head_size ** (-0.5) * LOG2E
    entries = head_count * pool_len

    storage = key_slot[tile_pool].reshape(head_count, seq_count, pool_len)
    by_reader = storage.transpose(1, 0, 2).reshape(seq_count, entries)
    ids = jnp.arange(entries, dtype=jnp.int32)
    before = (ids[:, None] < ids[None, :]).astype(jnp.bfloat16)
    wanted = by_reader // tile_count == me
    place = jnp.dot(
        wanted.astype(jnp.bfloat16), before, preferred_element_type=jnp.float32
    ).astype(jnp.int32)
    place = jnp.where(wanted, place, -1)
    code = (ids // pool_len)[None, :] * 65536 + by_reader % tile_count
    slots = jnp.arange(bound, dtype=jnp.int32)
    send = jnp.sum(
        jnp.where(place[:, None, :] == slots[None, :, None], code[:, None, :], 0), -1
    )

    own = lax.dynamic_index_in_dim(by_reader, me, 0, keepdims=False)
    owner = own // tile_count
    same = (owner[:, None] == owner[None, :]) & (ids[:, None] < ids[None, :])
    position = jnp.sum(same.astype(jnp.int32), 0)

    edges = chunk_edges(bound)
    chunks = []
    for lo, hi in zip(edges[:-1], edges[1:]):
        part = pack(send[:, lo:hi].reshape(-1), keys, values, head_size)
        part = part.reshape(seq_count, hi - lo, 2, TILE, head_size)
        got = lax.all_to_all(part, "seq", split_axis=0, concat_axis=0, tiled=True)
        chunks.append(got.reshape(-1, 2, TILE, head_size))

    head_ids = jnp.arange(head_count, dtype=jnp.int32)
    shared_codes = (
        head_ids[:, None] * 65536 + jnp.arange(SHARED, dtype=jnp.int32)[None, :]
    ).reshape(-1)
    shared_own = pack(shared_codes, keys, values, head_size)
    pieces = shared_own.reshape(seq_count, -1, head_size)
    piece = spread_shared(pieces, "seq")
    shared = lax.all_gather(piece, "seq", axis=0, tiled=True).reshape(
        head_count, SHARED, 2, TILE, head_size
    )

    listed = jnp.any(
        tile_lists[:, :, :, None] == jnp.arange(pool_len, dtype=jnp.int32), 2
    )
    bias = jnp.where(listed, 0.0, -FAR).astype(jnp.float32).transpose(0, 2, 1)
    bias = jnp.repeat(bias, TILE, axis=2)

    qt, acc, m, l = shared_part(queries, shared, head_count, head_size, scale)
    position = position.reshape(head_count, pool_len)
    owner = owner.reshape(head_count, pool_len)
    pool_ids = jnp.arange(pool_len, dtype=jnp.int32)
    state = (acc, m, l)
    for c, (lo, hi) in enumerate(zip(edges[:-1], edges[1:])):
        here = (position >= lo) & (position < hi)
        rank = jnp.sum(
            (here[:, :, None] & (pool_ids[:, None] < pool_ids[None, :])).astype(jnp.int32), 1
        )
        rank = jnp.where(here, rank, -1)
        hit = rank[:, None, :] == pool_ids[None, :, None]
        entry = jnp.sum(jnp.where(hit, pool_ids, 0), -1)
        where = owner * (hi - lo) + position - lo
        where = jnp.sum(jnp.where(hit, where[:, None, :], 0), -1)
        count = jnp.sum(here.astype(jnp.int32), 1)
        last = c == len(edges) - 2
        state = pool_part(
            (where, entry, count), qt, chunks[c], bias, *state, scale, last
        )
    return lax.all_to_all(state, "head", split_axis=0, concat_axis=1, tiled=True)


def solution(mesh):
    return jax.shard_map(
        body,
        mesh=mesh,
        in_specs=(
            P("seq", "head"),
            P("seq", "head"),
            P("seq", "head"),
            P("head", None),
            P("head", "seq", None),
            P(),
        ),
        out_specs=P(("seq", "head"), None),
        check_vma=False,
    )
```

```python
import functools

import jax
import jax.numpy as jnp
from jax import lax
from jax.experimental import pallas as pl
from jax.experimental.pallas import tpu as pltpu
from jax.sharding import PartitionSpec as P

TILE = 128
SHARED = 4
FAR = 1e30
LOG2E = 1.4426950408889634
VMEM_BYTES = 56 * 1024 * 1024


def pack_kernel(lo, bound, head_size, codes_ref, order_ref, keys_ref, values_ref, *out_refs):
    at = lo
    for out_ref in out_refs:
        readers = out_ref.shape[0] // bound

        def one(i, _):
            code = codes_ref[order_ref[at + i // bound] * bound + i % bound]
            rows = pl.ds(pl.multiple_of(code % 65536 * TILE, TILE), TILE)
            cols = pl.ds(pl.multiple_of(code // 65536 * head_size, head_size), head_size)
            out_ref[i, 0] = keys_ref[rows, cols]
            out_ref[i, 1] = values_ref[rows, cols]
            return 0

        lax.fori_loop(0, readers * bound, one, 0)
        at += readers


def pack(codes, order, keys, values, lo, sizes, bound, head_size):
    shapes = [
        jax.ShapeDtypeStruct((n * bound, 2, TILE, head_size), keys.dtype) for n in sizes
    ]
    whole = pl.BlockSpec(keys.shape, lambda i, *_: (0, 0))
    return pl.pallas_call(
        functools.partial(pack_kernel, lo, bound, head_size),
        grid_spec=pltpu.PrefetchScalarGridSpec(
            num_scalar_prefetch=2,
            grid=(1,),
            in_specs=[whole, whole],
            out_specs=[pl.BlockSpec(t.shape, lambda i, *_: (0, 0, 0, 0)) for t in shapes],
        ),
        out_shape=shapes,
        compiler_params=pltpu.CompilerParams(vmem_limit_bytes=VMEM_BYTES),
        name="pack_tiles",
    )(codes, order, keys, values)


def absorb(scale, block, k, vt, bias_row, qt_ref, acc_ref, m_ref, l_ref):
    for start in range(0, qt_ref.shape[2], block):
        cols = slice(start, start + block)
        s = jnp.dot(k, qt_ref[0, :, cols], preferred_element_type=jnp.float32)
        top = jnp.max(s, 0, keepdims=True) * scale
        m_old = m_ref[0, :, cols]
        if bias_row is None:
            m_new = jnp.maximum(m_old, top)
            shift = m_new
        else:
            bias = bias_row[:, cols]
            m_new = jnp.maximum(m_old, top + bias)
            shift = m_new - bias
        alpha = jnp.exp2(m_old - m_new)
        p = jnp.exp2(s * scale - shift)
        m_ref[0, :, cols] = m_new
        l_ref[0, :, cols] = l_ref[0, :, cols] * alpha + jnp.sum(p, 0, keepdims=True)
        acc_ref[0, :, cols] = acc_ref[0, :, cols] * alpha + jnp.dot(
            vt, p.astype(jnp.bfloat16), preferred_element_type=jnp.float32
        )


def shared_kernel(scale, block, qt_ref, k_ref, v_ref, acc_in, m_in, l_in, acc_ref, m_ref, l_ref):
    acc_ref[...] = acc_in[...]
    m_ref[...] = m_in[...]
    l_ref[...] = l_in[...]
    for j in range(SHARED):
        rows = slice(j * TILE, (j + 1) * TILE)
        absorb(
            scale, block, k_ref[rows, :], v_ref[rows, :].T, None, qt_ref, acc_ref, m_ref, l_ref
        )


def shared_part(qt, shared, state, scale):
    head_count, head_size, rows = qt.shape
    stat_spec = pl.BlockSpec((1, 1, rows), lambda h: (h, 0, 0))
    wide_spec = pl.BlockSpec((1, head_size, rows), lambda h: (h, 0, 0))
    keys = SHARED * TILE
    return pl.pallas_call(
        functools.partial(shared_kernel, scale, min(256, rows)),
        grid=(head_count,),
        out_shape=[jax.ShapeDtypeStruct(a.shape, a.dtype) for a in state],
        in_specs=[
            wide_spec,
            pl.BlockSpec((keys, head_size), lambda h: (0, h)),
            pl.BlockSpec((keys, head_size), lambda h: (1, h)),
            wide_spec,
            stat_spec,
            stat_spec,
        ],
        out_specs=[wide_spec, stat_spec, stat_spec],
        compiler_params=pltpu.CompilerParams(vmem_limit_bytes=VMEM_BYTES),
        name="shared_tiles",
    )(qt, shared, shared, *state)


def pool_kernel(
    scale, block, parts, first, split, head_lo,
    place_ref, entry_ref, count_ref, side_ref, q_ref, bias_ref, *refs,
):
    tiles = refs[:parts]
    held_ref, sems = refs[-2:]
    refs = refs[parts:-2]
    head = pl.program_id(0) + head_lo
    copies = []
    at = 0
    for k, tiles_ref in enumerate(tiles):
        span = pl.ds(at, tiles_ref.shape[0])
        copies.append(pltpu.make_async_copy(tiles_ref, held_ref.at[span], sems.at[k]))
        at += tiles_ref.shape[0]

    @pl.when(pl.program_id(0) == 0)
    def _():
        for copy in copies:
            copy.start()

    if first:
        qt_ref, acc_ref, m_ref, l_ref = refs
        qt_ref[0] = q_ref[...].T
        acc_ref[...] = jnp.zeros_like(acc_ref)
        m_ref[...] = jnp.full_like(m_ref, -0.5 * FAR)
        l_ref[...] = jnp.zeros_like(l_ref)
    else:
        qt_ref = q_ref
        acc_in, m_in, l_in = refs[:3]
        acc_ref, m_ref, l_ref = refs[-3:]
        acc_ref[...] = acc_in[...]
        m_ref[...] = m_in[...]
        l_ref[...] = l_in[...]

    @pl.when(pl.program_id(0) == 0)
    def _():
        for copy in copies:
            copy.wait()

    def one(i):
        place = place_ref[head, i]
        entry = entry_ref[head, i]
        absorb(
            scale, block, held_ref[place, 0], held_ref[place, 1].T,
            bias_ref[0, pl.ds(entry, 1), :], qt_ref, acc_ref, m_ref, l_ref,
        )

    def two(i, _):
        one(2 * i)
        one(2 * i + 1)
        return 0

    total = count_ref[head]
    lax.fori_loop(0, total // 2, two, 0)

    @pl.when(total % 2 == 1)
    def _():
        one(total - 1)

    if split:
        out_refs, whole = refs[3:-4], refs[-4]
        rows = qt_ref.shape[2]
        for start in range(0, rows, block):
            cols = slice(start, start + block)
            out = (acc_ref[0, :, cols] * (1.0 / l_ref[0, :, cols])).astype(jnp.bfloat16)
            whole[cols, :] = out.T
        if split == 1:
            out_refs[0][...] = whole[...]
        else:
            half = rows // split
            for ref, side in zip(out_refs, (side_ref[0], 1 - side_ref[0])):
                ref[...] = whole[pl.ds(pl.multiple_of(side * half, half), half), :]


def pool_part(tables, q, tiles, bias, state, scale, head_size, split=0, heads=None):
    first = state is None
    head_count, pool_len, rows = bias.shape
    lo, hi = heads or (0, head_count)
    count = hi - lo
    stat_spec = pl.BlockSpec((1, 1, rows), lambda h, *_: (h + lo, 0, 0))
    wide_spec = pl.BlockSpec((1, head_size, rows), lambda h, *_: (h + lo, 0, 0))
    acc = jax.ShapeDtypeStruct((head_count, head_size, rows), jnp.float32)
    stat = jax.ShapeDtypeStruct((head_count, 1, rows), jnp.float32)
    q_spec = pl.BlockSpec((rows, head_size), lambda h, *_: (0, h)) if first else wide_spec
    in_specs = [q_spec, pl.BlockSpec((1, pool_len, rows), lambda h, *_: (h + lo, 0, 0))]
    in_specs += [pl.BlockSpec(memory_space=pl.ANY)] * len(tiles)
    if not first:
        in_specs += [wide_spec, stat_spec, stat_spec]
    scratch = []
    if split:
        out_rows = rows // split
        out_shape = [
            jax.ShapeDtypeStruct((out_rows, count * head_size), jnp.bfloat16)
        ] * split
        out_specs = [pl.BlockSpec((out_rows, head_size), lambda h, *_: (0, h))] * split
        scratch = [
            pltpu.VMEM((rows, head_size), jnp.bfloat16),
            pltpu.VMEM((1, head_size, rows), jnp.float32),
            pltpu.VMEM((1, 1, rows), jnp.float32),
            pltpu.VMEM((1, 1, rows), jnp.float32),
        ]
    else:
        out_shape = [acc, stat, stat]
        out_specs = [wide_spec, stat_spec, stat_spec]
        if first:
            out_shape = [jax.ShapeDtypeStruct(acc.shape, jnp.bfloat16)] + out_shape
            out_specs = [wide_spec] + out_specs
    places = sum(t.shape[0] for t in tiles)
    scratch += [
        pltpu.VMEM((places, 2, TILE, head_size), jnp.bfloat16),
        pltpu.SemaphoreType.DMA((len(tiles),)),
    ]
    return pl.pallas_call(
        functools.partial(pool_kernel, scale, min(256, rows), len(tiles), first, split, lo),
        grid_spec=pltpu.PrefetchScalarGridSpec(
            num_scalar_prefetch=4,
            grid=(count,),
            in_specs=in_specs,
            out_specs=out_specs,
            scratch_shapes=scratch,
        ),
        out_shape=out_shape,
        compiler_params=pltpu.CompilerParams(vmem_limit_bytes=VMEM_BYTES),
        name="pool_tiles",
    )(*tables, q, bias, *tiles, *(() if first else state))


def scatter_shared(pieces, axis):
    me = lax.axis_index(axis)
    own = pieces[0]
    for k in range(1, pieces.shape[0]):
        own = jnp.where(me == k, lax.ppermute(pieces[k], axis, [(0, k)]), own)
    return own


def line_shared(own, size, axis):
    count = lax.axis_size(axis)
    me = lax.axis_index(axis)
    line = own
    for first in range(size, count, size):
        got = lax.ppermute(own, axis, [(k, first + k) for k in range(size)])
        line = jnp.where(me // size == first // size, got, line)
    return line


def body(queries, keys, values, tile_pool, tile_lists, key_slot):
    seq_count = lax.axis_size("seq")
    side_count = lax.axis_size("head")
    me = lax.axis_index("seq")
    side = lax.axis_index("head")
    head_count, pool_total = tile_pool.shape
    pool_len = pool_total // seq_count
    rows, width = queries.shape
    head_size = width // head_count
    tile_count = rows // TILE
    bound = (head_count * pool_len + seq_count - 1) // seq_count
    scale = head_size ** (-0.5) * LOG2E
    entries = head_count * pool_len

    stacked = jnp.concatenate([keys[: SHARED * TILE], values[: SHARED * TILE]], 0)
    stacked = stacked.reshape(min(4, seq_count), -1, width)

    tiles_all = jnp.arange(key_slot.shape[0], dtype=jnp.int32)
    storage = jnp.sum(
        jnp.where(tile_pool[:, :, None] == tiles_all, key_slot, 0), -1
    ).reshape(head_count, seq_count, pool_len)
    by_reader = storage.transpose(1, 0, 2).reshape(seq_count, entries)
    ids = jnp.arange(entries, dtype=jnp.int32)
    before = (ids[:, None] < ids[None, :]).astype(jnp.bfloat16)
    wanted = by_reader // tile_count == me
    place = jnp.dot(
        wanted.astype(jnp.bfloat16), before, preferred_element_type=jnp.float32
    ).astype(jnp.int32)
    place = jnp.where(wanted, place, -1)
    code = (ids // pool_len)[None, :] * 65536 + by_reader % tile_count
    slots = jnp.arange(bound, dtype=jnp.int32)
    send = jnp.sum(
        jnp.where(place[:, None, :] == slots[None, :, None], code[:, None, :], 0), -1
    ).reshape(-1)

    own = lax.dynamic_index_in_dim(by_reader, me, 0, keepdims=False)
    owner = own // tile_count
    same = (owner[:, None] == owner[None, :]) & (ids[:, None] < ids[None, :])
    position = jnp.sum(same.astype(jnp.int32), 0).reshape(head_count, pool_len)
    owner = owner.reshape(head_count, pool_len)
    pool_ids = jnp.arange(pool_len, dtype=jnp.int32)

    def listing(owners, bases):
        match = owner[:, :, None] == owners
        here = jnp.any(match, -1)
        base = jnp.sum(jnp.where(match, bases, 0), -1)
        rank = jnp.sum(
            (here[:, :, None] & (pool_ids[:, None] < pool_ids[None, :])).astype(jnp.int32), 1
        )
        rank = jnp.where(here, rank, -1)
        hit = rank[:, None, :] == pool_ids[None, :, None]
        entry = jnp.sum(jnp.where(hit, pool_ids, 0), -1)
        place = base + position
        place = jnp.sum(jnp.where(hit, place[:, None, :], 0), -1)
        return place, entry, jnp.sum(here.astype(jnp.int32), 1), side.reshape(1)

    half_count = seq_count // 2
    listed = jnp.any(
        tile_lists[:, :, :, None] == jnp.arange(pool_len, dtype=jnp.int32), 2
    )
    bias = jnp.where(listed, 0.0, -FAR).astype(jnp.float32).transpose(0, 2, 1)
    bias = jnp.repeat(bias, TILE, axis=2)
    split = 2 if side_count == 2 else 1
    part = functools.partial(pool_part, bias=bias, scale=scale, head_size=head_size)

    groups = [
        list(range(i, i + stacked.shape[0])) for i in range(0, seq_count, stacked.shape[0])
    ]

    if seq_count > 16:
        piece = line_shared(scatter_shared(stacked, "seq"), stacked.shape[0], "seq")
        shared = lax.all_gather(piece, "seq", axis=0, tiled=True, axis_index_groups=groups)
        everyone = jnp.arange(seq_count, dtype=jnp.int32)
        (sent,) = pack(send, everyone, keys, values, 0, [seq_count], bound, head_size)
        got = lax.all_to_all(sent, "seq", split_axis=0, concat_axis=0, tiled=True)
        tables = listing(everyone, everyone * bound)
        qt, *state = part(tables, queries, [got], state=None)
        state = shared_part(qt, shared, state, scale)
        tables = (*tables[:2], 0 * tables[2], tables[3])
        last = functools.partial(part, tables, qt, [got], state=state)
    else:
        order = [4, 8, 5, 9, 1, 2, 6, 10, 3, 7, 11, 12, 13, 14, 15, 0]
        partners = me ^ jnp.asarray(order, jnp.int32)
        where = {d: i for i, d in enumerate(order)}

        def use(state, blocks, ds, **kwargs):
            owners = jnp.stack([partners[where[d]] for d in ds])
            tables = listing(owners, bound * jnp.arange(len(ds)))
            q = queries if state is None else qt
            return part(tables, q, [blocks[d] for d in ds], state=state, **kwargs)

        def move(ds):
            return {
                d: lax.ppermute(parts[d], "seq", [(j, j ^ d) for j in range(seq_count)])
                for d in ds
            }

        def fence(*values):
            return lax.optimization_barrier(values)

        head_start = 4
        parts = list(pack(send, partners, keys, values, 0, [1] * head_start, bound, head_size))
        stacked, parts[0] = fence(stacked, parts[0])
        rest = len(order) - head_start
        parts += pack(send, partners, keys, values, head_start, [1] * rest, bound, head_size)
        parts = dict(zip(order, parts))

        piece = scatter_shared(stacked, "seq")
        first = order[:11]
        got = move([4, 8])
        held = [parts[d] for d in (5, 9, 1)]
        *held, piece = fence(*held, piece)
        parts.update(zip((5, 9, 1), held))
        got.update(move([5, 9, 1]))
        for d, earlier in ((6, 4), (10, 8), (2, 1), (7, 5), (11, 9), (3, 2)):
            parts[d], got[earlier] = fence(parts[d], got[earlier])
            got.update(move([d]))
        quarter = stacked.shape[0]
        piece, got[6] = fence(piece, got[6])
        over = lax.ppermute(piece, "seq", [(k, half_count + k) for k in range(quarter)])
        qt, *state = use(None, parts, [0])
        parts, got, piece, over, qt, state = fence(parts, got, piece, over, qt, state)

        halves = [list(range(half_count)), list(range(half_count, seq_count))]
        piece = jnp.where(me >= half_count, over, piece)
        shared = lax.all_gather(piece, "seq", axis=0, tiled=True, axis_index_groups=halves)
        new = move([12, 13, 14, 15])
        state = use(state, got, first)
        state = shared_part(qt, shared, state, scale)
        state = use(state, new, [12, 13])
        state = use(state, new, [14])
        last = functools.partial(use, state, new, [15])

    if split == 1:
        (out,) = last(split=1)
        return lax.all_to_all(out, "head", split_axis=0, concat_axis=1, tiled=True)

    half = head_count // 2
    result = jnp.zeros((rows // 2, 2 * width), jnp.bfloat16)
    kept = []
    arrived = []
    for lo, hi in ((0, half), (half, head_count)):
        keep, away = last(split=2, heads=(lo, hi))
        kept.append((lo, keep))
        arrived.append((lo, lax.ppermute(away, "head", [(0, 1), (1, 0)])))
    for lo, block in kept:
        result = lax.dynamic_update_slice(result, block, (0, side * width + lo * head_size))
    for lo, block in arrived:
        result = lax.dynamic_update_slice(
            result, block, (0, (1 - side) * width + lo * head_size)
        )
    return result


def solution(mesh):
    return jax.shard_map(
        body,
        mesh=mesh,
        in_specs=(
            P("seq", "head"),
            P("seq", "head"),
            P("seq", "head"),
            P("head", None),
            P("head", "seq", None),
            P(),
        ),
        out_specs=P(("seq", "head"), None),
        check_vma=False,
    )
```

```python
import functools

import jax
import jax.numpy as jnp
from jax import lax
from jax.experimental import pallas as pl
from jax.experimental.pallas import tpu as pltpu
from jax.sharding import PartitionSpec as P

TILE = 128
SHARED = 4
FAR = 1e30
LOG2E = 1.4426950408889634
VMEM_BYTES = 56 * 1024 * 1024
WORK_BYTES = 12 * 1024 * 1024


def pack_kernel(lo, bound, head_size, codes_ref, order_ref, keys_ref, values_ref, *out_refs):
    at = lo
    for out_ref in out_refs:
        readers = out_ref.shape[0] // bound

        def one(i, _):
            code = codes_ref[order_ref[at + i // bound] * bound + i % bound]
            rows = pl.ds(pl.multiple_of(code % 65536 * TILE, TILE), TILE)
            cols = pl.ds(pl.multiple_of(code // 65536 * head_size, head_size), head_size)
            out_ref[i, 0] = keys_ref[rows, cols]
            out_ref[i, 1] = values_ref[rows, cols]
            return 0

        lax.fori_loop(0, readers * bound, one, 0)
        at += readers


def pack(codes, order, keys, values, lo, sizes, bound, head_size):
    shapes = [
        jax.ShapeDtypeStruct((n * bound, 2, TILE, head_size), keys.dtype) for n in sizes
    ]
    whole = pl.BlockSpec(keys.shape, lambda i, *_: (0, 0))
    return pl.pallas_call(
        functools.partial(pack_kernel, lo, bound, head_size),
        grid_spec=pltpu.PrefetchScalarGridSpec(
            num_scalar_prefetch=2,
            grid=(1,),
            in_specs=[whole, whole],
            out_specs=[pl.BlockSpec(t.shape, lambda i, *_: (0, 0, 0, 0)) for t in shapes],
        ),
        out_shape=shapes,
        compiler_params=pltpu.CompilerParams(vmem_limit_bytes=VMEM_BYTES),
        name="pack_tiles",
    )(codes, order, keys, values)


def absorb(scale, block, k, vt, bias_row, qt_ref, acc_ref, m_ref, l_ref):
    for start in range(0, qt_ref.shape[2], block):
        cols = slice(start, start + block)
        s = jnp.dot(k, qt_ref[0, :, cols], preferred_element_type=jnp.float32)
        top = jnp.max(s, 0, keepdims=True) * scale
        m_old = m_ref[0, :, cols]
        if bias_row is None:
            m_new = jnp.maximum(m_old, top)
            shift = m_new
        else:
            bias = bias_row[:, cols]
            m_new = jnp.maximum(m_old, top + bias)
            shift = m_new - bias
        alpha = jnp.exp2(m_old - m_new)
        p = jnp.exp2(s * scale - shift)
        m_ref[0, :, cols] = m_new
        l_ref[0, :, cols] = l_ref[0, :, cols] * alpha + jnp.sum(p, 0, keepdims=True)
        acc_ref[0, :, cols] = acc_ref[0, :, cols] * alpha + jnp.dot(
            vt, p.astype(jnp.bfloat16), preferred_element_type=jnp.float32
        )


def shared_kernel(scale, block, qt_ref, k_ref, v_ref, acc_in, m_in, l_in, acc_ref, m_ref, l_ref):
    acc_ref[...] = acc_in[...]
    m_ref[...] = m_in[...]
    l_ref[...] = l_in[...]
    for j in range(SHARED):
        rows = slice(j * TILE, (j + 1) * TILE)
        absorb(
            scale, block, k_ref[rows, :], v_ref[rows, :].T, None, qt_ref, acc_ref, m_ref, l_ref
        )


def shared_part(qt, shared, state, scale):
    head_count, head_size, rows = qt.shape
    stat_spec = pl.BlockSpec((1, 1, rows), lambda h: (h, 0, 0))
    wide_spec = pl.BlockSpec((1, head_size, rows), lambda h: (h, 0, 0))
    keys = SHARED * TILE
    return pl.pallas_call(
        functools.partial(shared_kernel, scale, min(256, rows)),
        grid=(head_count,),
        out_shape=[jax.ShapeDtypeStruct(a.shape, a.dtype) for a in state],
        in_specs=[
            wide_spec,
            pl.BlockSpec((keys, head_size), lambda h: (0, h)),
            pl.BlockSpec((keys, head_size), lambda h: (2, h)),
            wide_spec,
            stat_spec,
            stat_spec,
        ],
        out_specs=[wide_spec, stat_spec, stat_spec],
        compiler_params=pltpu.CompilerParams(vmem_limit_bytes=WORK_BYTES),
        name="shared_tiles",
    )(qt, shared, shared, *state)


def pool_kernel(
    scale, block, parts, first, split, head_lo,
    place_ref, entry_ref, count_ref, side_ref, q_ref, bias_ref, *refs,
):
    tiles = refs[:parts]
    held_ref, sems = refs[-2:]
    refs = refs[parts:-2]
    head = pl.program_id(0) + head_lo
    copies = []
    at = 0
    for k, tiles_ref in enumerate(tiles):
        span = pl.ds(at, tiles_ref.shape[0])
        copies.append(pltpu.make_async_copy(tiles_ref, held_ref.at[span], sems.at[k]))
        at += tiles_ref.shape[0]

    @pl.when(pl.program_id(0) == 0)
    def _():
        for copy in copies:
            copy.start()

    if first:
        qt_ref, acc_ref, m_ref, l_ref = refs
        qt_ref[0] = q_ref[...].T
        acc_ref[...] = jnp.zeros_like(acc_ref)
        m_ref[...] = jnp.full_like(m_ref, -0.5 * FAR)
        l_ref[...] = jnp.zeros_like(l_ref)
    else:
        qt_ref = q_ref
        acc_in, m_in, l_in = refs[:3]
        acc_ref, m_ref, l_ref = refs[-3:]
        acc_ref[...] = acc_in[...]
        m_ref[...] = m_in[...]
        l_ref[...] = l_in[...]

    @pl.when(pl.program_id(0) == 0)
    def _():
        for copy in copies:
            copy.wait()

    def one(i):
        place = place_ref[head, i]
        entry = entry_ref[head, i]
        absorb(
            scale, block, held_ref[place, 0], held_ref[place, 1].T,
            bias_ref[0, pl.ds(entry, 1), :], qt_ref, acc_ref, m_ref, l_ref,
        )

    def two(i, _):
        one(2 * i)
        one(2 * i + 1)
        return 0

    total = count_ref[head]
    lax.fori_loop(0, total // 2, two, 0)

    @pl.when(total % 2 == 1)
    def _():
        one(total - 1)

    if split:
        out_refs, whole = refs[3:-4], refs[-4]
        rows = qt_ref.shape[2]
        for start in range(0, rows, block):
            cols = slice(start, start + block)
            out = (acc_ref[0, :, cols] * (1.0 / l_ref[0, :, cols])).astype(jnp.bfloat16)
            whole[cols, :] = out.T
        if split == 1:
            out_refs[0][...] = whole[...]
        else:
            half = rows // split
            for ref, side in zip(out_refs, (side_ref[0], 1 - side_ref[0])):
                ref[...] = whole[pl.ds(pl.multiple_of(side * half, half), half), :]


def pool_part(tables, q, tiles, bias, state, scale, head_size, split=0, heads=None):
    first = state is None
    head_count, pool_len, rows = bias.shape
    lo, hi = heads or (0, head_count)
    count = hi - lo
    stat_spec = pl.BlockSpec((1, 1, rows), lambda h, *_: (h + lo, 0, 0))
    wide_spec = pl.BlockSpec((1, head_size, rows), lambda h, *_: (h + lo, 0, 0))
    acc = jax.ShapeDtypeStruct((head_count, head_size, rows), jnp.float32)
    stat = jax.ShapeDtypeStruct((head_count, 1, rows), jnp.float32)
    q_spec = pl.BlockSpec((rows, head_size), lambda h, *_: (0, h)) if first else wide_spec
    in_specs = [q_spec, pl.BlockSpec((1, pool_len, rows), lambda h, *_: (h + lo, 0, 0))]
    in_specs += [pl.BlockSpec(memory_space=pl.ANY)] * len(tiles)
    if not first:
        in_specs += [wide_spec, stat_spec, stat_spec]
    scratch = []
    if split:
        out_rows = rows // split
        out_shape = [
            jax.ShapeDtypeStruct((out_rows, count * head_size), jnp.bfloat16)
        ] * split
        out_specs = [pl.BlockSpec((out_rows, head_size), lambda h, *_: (0, h))] * split
        scratch = [
            pltpu.VMEM((rows, head_size), jnp.bfloat16),
            pltpu.VMEM((1, head_size, rows), jnp.float32),
            pltpu.VMEM((1, 1, rows), jnp.float32),
            pltpu.VMEM((1, 1, rows), jnp.float32),
        ]
    else:
        out_shape = [acc, stat, stat]
        out_specs = [wide_spec, stat_spec, stat_spec]
        if first:
            out_shape = [jax.ShapeDtypeStruct(acc.shape, jnp.bfloat16)] + out_shape
            out_specs = [wide_spec] + out_specs
    places = sum(t.shape[0] for t in tiles)
    scratch += [
        pltpu.VMEM((places, 2, TILE, head_size), jnp.bfloat16),
        pltpu.SemaphoreType.DMA((len(tiles),)),
    ]
    return pl.pallas_call(
        functools.partial(pool_kernel, scale, min(256, rows), len(tiles), first, split, lo),
        grid_spec=pltpu.PrefetchScalarGridSpec(
            num_scalar_prefetch=4,
            grid=(count,),
            in_specs=in_specs,
            out_specs=out_specs,
            scratch_shapes=scratch,
        ),
        out_shape=out_shape,
        compiler_params=pltpu.CompilerParams(
            vmem_limit_bytes=WORK_BYTES + places * 2 * TILE * head_size * 2
        ),
        name="pool_tiles",
    )(*tables, q, bias, *tiles, *(() if first else state))


def share_halves(keys, values, axis, size):
    me = lax.axis_index(axis)
    got = lax.ppermute(values, axis, [(0, size // 2)])
    return jnp.where(me % size == size // 2, got, keys)


def share_step(piece, axis, size, step):
    count = lax.axis_size(axis)
    me = lax.axis_index(axis)
    pairs = [
        (j + k, j + k + step) for j in range(0, count, 2 * step) for k in (0, size // 2)
    ]
    over = lax.ppermute(piece, axis, pairs)
    return jnp.where(me // step % 2 == 1, over, piece)


def share_within(piece, axis, size):
    groups = [list(range(i, i + size)) for i in range(0, lax.axis_size(axis), size)]
    return lax.all_gather(piece, axis, axis=0, tiled=True, axis_index_groups=groups)


def body(queries, keys, values, tile_pool, tile_lists, key_slot):
    seq_count = lax.axis_size("seq")
    side_count = lax.axis_size("head")
    me = lax.axis_index("seq")
    side = lax.axis_index("head")
    head_count, pool_total = tile_pool.shape
    pool_len = pool_total // seq_count
    rows, width = queries.shape
    head_size = width // head_count
    tile_count = rows // TILE
    bound = (head_count * pool_len + seq_count - 1) // seq_count
    scale = head_size ** (-0.5) * LOG2E
    entries = head_count * pool_len

    shared_keys, shared_values = keys[: SHARED * TILE], values[: SHARED * TILE]
    quarter = 4

    tiles_all = jnp.arange(key_slot.shape[0], dtype=jnp.int32)
    storage = jnp.sum(
        jnp.where(tile_pool[:, :, None] == tiles_all, key_slot, 0), -1
    ).reshape(head_count, seq_count, pool_len)
    by_reader = storage.transpose(1, 0, 2).reshape(seq_count, entries)
    ids = jnp.arange(entries, dtype=jnp.int32)
    before = (ids[:, None] < ids[None, :]).astype(jnp.bfloat16)
    wanted = by_reader // tile_count == me
    place = jnp.dot(
        wanted.astype(jnp.bfloat16), before, preferred_element_type=jnp.float32
    ).astype(jnp.int32)
    place = jnp.where(wanted, place, -1)
    code = (ids // pool_len)[None, :] * 65536 + by_reader % tile_count
    slots = jnp.arange(bound, dtype=jnp.int32)
    send = jnp.sum(
        jnp.where(place[:, None, :] == slots[None, :, None], code[:, None, :], 0), -1
    ).reshape(-1)

    own = lax.dynamic_index_in_dim(by_reader, me, 0, keepdims=False)
    owner = own // tile_count
    same = (owner[:, None] == owner[None, :]) & (ids[:, None] < ids[None, :])
    position = jnp.sum(same.astype(jnp.int32), 0).reshape(head_count, pool_len)
    owner = owner.reshape(head_count, pool_len)
    pool_ids = jnp.arange(pool_len, dtype=jnp.int32)

    def listing(owners, bases):
        match = owner[:, :, None] == owners
        here = jnp.any(match, -1)
        base = jnp.sum(jnp.where(match, bases, 0), -1)
        rank = jnp.sum(
            (here[:, :, None] & (pool_ids[:, None] < pool_ids[None, :])).astype(jnp.int32), 1
        )
        rank = jnp.where(here, rank, -1)
        hit = rank[:, None, :] == pool_ids[None, :, None]
        entry = jnp.sum(jnp.where(hit, pool_ids, 0), -1)
        place = base + position
        place = jnp.sum(jnp.where(hit, place[:, None, :], 0), -1)
        return place, entry, jnp.sum(here.astype(jnp.int32), 1), side.reshape(1)

    half_count = seq_count // 2
    listed = jnp.any(
        tile_lists[:, :, :, None] == jnp.arange(pool_len, dtype=jnp.int32), 2
    )
    bias = jnp.where(listed, 0.0, -FAR).astype(jnp.float32).transpose(0, 2, 1)
    bias = jnp.repeat(bias, TILE, axis=2)
    split = 2 if side_count == 2 else 1
    part = functools.partial(pool_part, bias=bias, scale=scale, head_size=head_size)

    if seq_count > 16:
        piece = share_halves(shared_keys, shared_values, "seq", quarter)
        step = seq_count // 2
        while step >= quarter:
            piece = share_step(piece, "seq", quarter, step)
            step //= 2
        shared = share_within(piece, "seq", quarter)
        everyone = jnp.arange(seq_count, dtype=jnp.int32)
        (sent,) = pack(send, everyone, keys, values, 0, [seq_count], bound, head_size)
        got = lax.all_to_all(sent, "seq", split_axis=0, concat_axis=0, tiled=True)
        tables = listing(everyone, everyone * bound)
        qt, *state = part(tables, queries, [got], state=None)
        state = shared_part(qt, shared, state, scale)
        tables = (*tables[:2], 0 * tables[2], tables[3])
        last = functools.partial(part, tables, qt, [got], state=state)
    else:
        order = [4, 8, 5, 9, 1, 2, 10, 3, 11, 7, 6, 12, 13, 14, 15, 0]
        partners = me ^ jnp.asarray(order, jnp.int32)
        where = {d: i for i, d in enumerate(order)}

        def use(state, blocks, ds, **kwargs):
            owners = jnp.stack([partners[where[d]] for d in ds])
            tables = listing(owners, bound * jnp.arange(len(ds)))
            q = queries if state is None else qt
            return part(tables, q, [blocks[d] for d in ds], state=state, **kwargs)

        def move(ds):
            return {
                d: lax.ppermute(parts[d], "seq", [(j, j ^ d) for j in range(seq_count)])
                for d in ds
            }

        def fence(*values):
            return lax.optimization_barrier(values)

        parts = {}
        for lo, hi in ((0, 4), (4, 10), (10, len(order))):
            packed = pack(send, partners, keys, values, lo, [1] * (hi - lo), bound, head_size)
            parts.update(zip(order[lo:hi], packed))

        piece = share_halves(shared_keys, shared_values, "seq", quarter)
        first = [5, 1, 2, 10, 3, 11, 7]
        got = move([4, 8, 5, 9])
        piece, parts[4] = fence(piece, parts[4])
        piece = share_step(piece, "seq", quarter, half_count)
        for d, earlier in ((1, 4), (10, 8), (2, 1), (11, 9), (3, 2), (7, 5)):
            parts[d], got[earlier] = fence(parts[d], got[earlier])
            got.update(move([d]))
        piece = share_step(piece, "seq", quarter, quarter)
        got[0] = parts[0]
        qt, *state = use(None, got, [0, 4, 8, 9])
        parts, got, piece, qt, state = fence(parts, got, piece, qt, state)

        shared = share_within(piece, "seq", quarter)
        new = move([6, 12, 13, 14, 15])
        state = use(state, got, first)
        state = shared_part(qt, shared, state, scale)
        state = use(state, new, [6, 12, 13])
        state = use(state, new, [14])
        last = functools.partial(use, state, new, [15])

    if split == 1:
        (out,) = last(split=1)
        return lax.all_to_all(out, "head", split_axis=0, concat_axis=1, tiled=True)

    third = head_count // 3
    result = jnp.zeros((rows // 2, 2 * width), jnp.bfloat16)
    kept = []
    arrived = []
    for lo, hi in ((0, third), (third, 2 * third), (2 * third, head_count)):
        keep, away = last(split=2, heads=(lo, hi))
        kept.append((lo, keep))
        arrived.append((lo, lax.ppermute(away, "head", [(0, 1), (1, 0)])))
    for lo, block in kept:
        result = lax.dynamic_update_slice(result, block, (0, side * width + lo * head_size))
    for lo, block in arrived:
        result = lax.dynamic_update_slice(
            result, block, (0, (1 - side) * width + lo * head_size)
        )
    return result


def solution(mesh):
    return jax.shard_map(
        body,
        mesh=mesh,
        in_specs=(
            P("seq", "head"),
            P("seq", "head"),
            P("seq", "head"),
            P("head", None),
            P("head", "seq", None),
            P(),
        ),
        out_specs=P(("seq", "head"), None),
        check_vma=False,
    )
```

```python
import functools

import jax
import jax.numpy as jnp
from jax import lax
from jax.experimental import pallas as pl
from jax.experimental.pallas import tpu as pltpu
from jax.sharding import PartitionSpec as P

TILE = 128
SHARED = 4
FAR = 1e30
LOG2E = 1.4426950408889634
VMEM_BYTES = 56 * 1024 * 1024
WORK_BYTES = 12 * 1024 * 1024


def pack_kernel(lo, bound, head_size, codes_ref, order_ref, keys_ref, values_ref, *out_refs):
    at = lo
    for out_ref in out_refs:
        readers = out_ref.shape[0] // bound

        def one(i, _):
            code = codes_ref[order_ref[at + i // bound] * bound + i % bound]
            rows = pl.ds(pl.multiple_of(code % 65536 * TILE, TILE), TILE)
            cols = pl.ds(pl.multiple_of(code // 65536 * head_size, head_size), head_size)
            out_ref[i, 0] = keys_ref[rows, cols]
            out_ref[i, 1] = values_ref[rows, cols]
            return 0

        lax.fori_loop(0, readers * bound, one, 0)
        at += readers


def pack(codes, order, keys, values, lo, sizes, bound, head_size):
    shapes = [
        jax.ShapeDtypeStruct((n * bound, 2, TILE, head_size), keys.dtype) for n in sizes
    ]
    whole = pl.BlockSpec(keys.shape, lambda i, *_: (0, 0))
    return pl.pallas_call(
        functools.partial(pack_kernel, lo, bound, head_size),
        grid_spec=pltpu.PrefetchScalarGridSpec(
            num_scalar_prefetch=2,
            grid=(1,),
            in_specs=[whole, whole],
            out_specs=[pl.BlockSpec(t.shape, lambda i, *_: (0, 0, 0, 0)) for t in shapes],
        ),
        out_shape=shapes,
        compiler_params=pltpu.CompilerParams(vmem_limit_bytes=VMEM_BYTES),
        name="pack_tiles",
    )(codes, order, keys, values)


def absorb(scale, block, k, vt, bias_row, qt_ref, acc_ref, m_ref, l_ref):
    for start in range(0, qt_ref.shape[2], block):
        cols = slice(start, start + block)
        s = jnp.dot(k, qt_ref[0, :, cols], preferred_element_type=jnp.float32)
        top = jnp.max(s, 0, keepdims=True) * scale
        m_old = m_ref[0, :, cols]
        if bias_row is None:
            m_new = jnp.maximum(m_old, top)
            shift = m_new
        else:
            bias = bias_row[:, cols]
            m_new = jnp.maximum(m_old, top + bias)
            shift = m_new - bias
        alpha = jnp.exp2(m_old - m_new)
        p = jnp.exp2(s * scale - shift)
        m_ref[0, :, cols] = m_new
        l_ref[0, :, cols] = l_ref[0, :, cols] * alpha + jnp.sum(p, 0, keepdims=True)
        acc_ref[0, :, cols] = acc_ref[0, :, cols] * alpha + jnp.dot(
            vt, p.astype(jnp.bfloat16), preferred_element_type=jnp.float32
        )


def shared_kernel(scale, block, qt_ref, k_ref, v_ref, acc_in, m_in, l_in, acc_ref, m_ref, l_ref):
    acc_ref[...] = acc_in[...]
    m_ref[...] = m_in[...]
    l_ref[...] = l_in[...]
    for j in range(SHARED):
        rows = slice(j * TILE, (j + 1) * TILE)
        absorb(
            scale, block, k_ref[rows, :], v_ref[rows, :].T, None, qt_ref, acc_ref, m_ref, l_ref
        )


def shared_part(qt, shared, state, scale):
    head_count, head_size, rows = qt.shape
    stat_spec = pl.BlockSpec((1, 1, rows), lambda h: (h, 0, 0))
    wide_spec = pl.BlockSpec((1, head_size, rows), lambda h: (h, 0, 0))
    keys = SHARED * TILE
    return pl.pallas_call(
        functools.partial(shared_kernel, scale, min(256, rows)),
        grid=(head_count,),
        out_shape=[jax.ShapeDtypeStruct(a.shape, a.dtype) for a in state],
        in_specs=[
            wide_spec,
            pl.BlockSpec((keys, head_size), lambda h: (0, h)),
            pl.BlockSpec((keys, head_size), lambda h: (2, h)),
            wide_spec,
            stat_spec,
            stat_spec,
        ],
        out_specs=[wide_spec, stat_spec, stat_spec],
        compiler_params=pltpu.CompilerParams(vmem_limit_bytes=WORK_BYTES),
        name="shared_tiles",
    )(qt, shared, shared, *state)


def pool_kernel(
    scale, block, parts, first, split, head_lo,
    place_ref, entry_ref, count_ref, side_ref, q_ref, bias_ref, *refs,
):
    tiles = refs[:parts]
    held_ref, sems = refs[-2:]
    refs = refs[parts:-2]
    head = pl.program_id(0) + head_lo
    copies = []
    at = 0
    for k, tiles_ref in enumerate(tiles):
        span = pl.ds(at, tiles_ref.shape[0])
        copies.append(pltpu.make_async_copy(tiles_ref, held_ref.at[span], sems.at[k]))
        at += tiles_ref.shape[0]

    @pl.when(pl.program_id(0) == 0)
    def _():
        for copy in copies:
            copy.start()

    if first:
        qt_ref, acc_ref, m_ref, l_ref = refs
        qt_ref[0] = q_ref[...].T
        acc_ref[...] = jnp.zeros_like(acc_ref)
        m_ref[...] = jnp.full_like(m_ref, -0.5 * FAR)
        l_ref[...] = jnp.zeros_like(l_ref)
    else:
        qt_ref = q_ref
        acc_in, m_in, l_in = refs[:3]
        acc_ref, m_ref, l_ref = refs[-3:]
        acc_ref[...] = acc_in[...]
        m_ref[...] = m_in[...]
        l_ref[...] = l_in[...]

    @pl.when(pl.program_id(0) == 0)
    def _():
        for copy in copies:
            copy.wait()

    def one(i):
        place = place_ref[head, i]
        entry = entry_ref[head, i]
        absorb(
            scale, block, held_ref[place, 0], held_ref[place, 1].T,
            bias_ref[0, pl.ds(entry, 1), :], qt_ref, acc_ref, m_ref, l_ref,
        )

    def two(i, _):
        one(2 * i)
        one(2 * i + 1)
        return 0

    total = count_ref[head]
    lax.fori_loop(0, total // 2, two, 0)

    @pl.when(total % 2 == 1)
    def _():
        one(total - 1)

    if split:
        out_refs, whole = refs[3:-4], refs[-4]
        rows = qt_ref.shape[2]
        for start in range(0, rows, block):
            cols = slice(start, start + block)
            out = (acc_ref[0, :, cols] * (1.0 / l_ref[0, :, cols])).astype(jnp.bfloat16)
            whole[cols, :] = out.T
        if split == 1:
            out_refs[0][...] = whole[...]
        else:
            half = rows // split
            for ref, side in zip(out_refs, (side_ref[0], 1 - side_ref[0])):
                ref[...] = whole[pl.ds(pl.multiple_of(side * half, half), half), :]


def pool_part(tables, q, tiles, bias, state, scale, head_size, split=0, heads=None):
    first = state is None
    head_count, pool_len, rows = bias.shape
    lo, hi = heads or (0, head_count)
    count = hi - lo
    stat_spec = pl.BlockSpec((1, 1, rows), lambda h, *_: (h + lo, 0, 0))
    wide_spec = pl.BlockSpec((1, head_size, rows), lambda h, *_: (h + lo, 0, 0))
    acc = jax.ShapeDtypeStruct((head_count, head_size, rows), jnp.float32)
    stat = jax.ShapeDtypeStruct((head_count, 1, rows), jnp.float32)
    q_spec = pl.BlockSpec((rows, head_size), lambda h, *_: (0, h)) if first else wide_spec
    in_specs = [q_spec, pl.BlockSpec((1, pool_len, rows), lambda h, *_: (h + lo, 0, 0))]
    in_specs += [pl.BlockSpec(memory_space=pl.ANY)] * len(tiles)
    if not first:
        in_specs += [wide_spec, stat_spec, stat_spec]
    scratch = []
    if split:
        out_rows = rows // split
        out_shape = [
            jax.ShapeDtypeStruct((out_rows, count * head_size), jnp.bfloat16)
        ] * split
        out_specs = [pl.BlockSpec((out_rows, head_size), lambda h, *_: (0, h))] * split
        scratch = [
            pltpu.VMEM((rows, head_size), jnp.bfloat16),
            pltpu.VMEM((1, head_size, rows), jnp.float32),
            pltpu.VMEM((1, 1, rows), jnp.float32),
            pltpu.VMEM((1, 1, rows), jnp.float32),
        ]
    else:
        out_shape = [acc, stat, stat]
        out_specs = [wide_spec, stat_spec, stat_spec]
        if first:
            out_shape = [jax.ShapeDtypeStruct(acc.shape, jnp.bfloat16)] + out_shape
            out_specs = [wide_spec] + out_specs
    places = sum(t.shape[0] for t in tiles)
    scratch += [
        pltpu.VMEM((places, 2, TILE, head_size), jnp.bfloat16),
        pltpu.SemaphoreType.DMA((len(tiles),)),
    ]
    return pl.pallas_call(
        functools.partial(pool_kernel, scale, min(256, rows), len(tiles), first, split, lo),
        grid_spec=pltpu.PrefetchScalarGridSpec(
            num_scalar_prefetch=4,
            grid=(count,),
            in_specs=in_specs,
            out_specs=out_specs,
            scratch_shapes=scratch,
        ),
        out_shape=out_shape,
        compiler_params=pltpu.CompilerParams(
            vmem_limit_bytes=WORK_BYTES + places * 2 * TILE * head_size * 2
        ),
        name="pool_tiles",
    )(*tables, q, bias, *tiles, *(() if first else state))


def share_halves(keys, values, axis, size):
    me = lax.axis_index(axis)
    got = lax.ppermute(values, axis, [(0, size // 2)])
    return jnp.where(me % size == size // 2, got, keys)


def share_step(piece, axis, size, step):
    count = lax.axis_size(axis)
    me = lax.axis_index(axis)
    pairs = [
        (j + k, j + k + step) for j in range(0, count, 2 * step) for k in (0, size // 2)
    ]
    over = lax.ppermute(piece, axis, pairs)
    return jnp.where(me // step % 2 == 1, over, piece)


def share_within(piece, axis, size):
    groups = [list(range(i, i + size)) for i in range(0, lax.axis_size(axis), size)]
    return lax.all_gather(piece, axis, axis=0, tiled=True, axis_index_groups=groups)


def body(queries, keys, values, tile_pool, tile_lists, key_slot):
    seq_count = lax.axis_size("seq")
    side_count = lax.axis_size("head")
    me = lax.axis_index("seq")
    side = lax.axis_index("head")
    head_count, pool_total = tile_pool.shape
    pool_len = pool_total // seq_count
    rows, width = queries.shape
    head_size = width // head_count
    tile_count = rows // TILE
    bound = (head_count * pool_len + seq_count - 1) // seq_count
    scale = head_size ** (-0.5) * LOG2E
    entries = head_count * pool_len

    shared_keys, shared_values = keys[: SHARED * TILE], values[: SHARED * TILE]
    quarter = 4

    tiles_all = jnp.arange(key_slot.shape[0], dtype=jnp.int32)
    storage = jnp.sum(
        jnp.where(tile_pool[:, :, None] == tiles_all, key_slot, 0), -1
    ).reshape(head_count, seq_count, pool_len)
    by_reader = storage.transpose(1, 0, 2).reshape(seq_count, entries)
    ids = jnp.arange(entries, dtype=jnp.int32)
    before = (ids[:, None] < ids[None, :]).astype(jnp.bfloat16)
    wanted = by_reader // tile_count == me
    place = jnp.dot(
        wanted.astype(jnp.bfloat16), before, preferred_element_type=jnp.float32
    ).astype(jnp.int32)
    place = jnp.where(wanted, place, -1)
    code = (ids // pool_len)[None, :] * 65536 + by_reader % tile_count
    slots = jnp.arange(bound, dtype=jnp.int32)
    send = jnp.sum(
        jnp.where(place[:, None, :] == slots[None, :, None], code[:, None, :], 0), -1
    ).reshape(-1)

    own = lax.dynamic_index_in_dim(by_reader, me, 0, keepdims=False)
    owner = own // tile_count
    same = (owner[:, None] == owner[None, :]) & (ids[:, None] < ids[None, :])
    position = jnp.sum(same.astype(jnp.int32), 0).reshape(head_count, pool_len)
    owner = owner.reshape(head_count, pool_len)
    pool_ids = jnp.arange(pool_len, dtype=jnp.int32)

    def listing(owners, bases):
        match = owner[:, :, None] == owners
        here = jnp.any(match, -1)
        base = jnp.sum(jnp.where(match, bases, 0), -1)
        rank = jnp.sum(
            (here[:, :, None] & (pool_ids[:, None] < pool_ids[None, :])).astype(jnp.int32), 1
        )
        rank = jnp.where(here, rank, -1)
        hit = rank[:, None, :] == pool_ids[None, :, None]
        entry = jnp.sum(jnp.where(hit, pool_ids, 0), -1)
        place = base + position
        place = jnp.sum(jnp.where(hit, place[:, None, :], 0), -1)
        return place, entry, jnp.sum(here.astype(jnp.int32), 1), side.reshape(1)

    half_count = seq_count // 2
    listed = jnp.any(
        tile_lists[:, :, :, None] == jnp.arange(pool_len, dtype=jnp.int32), 2
    )
    bias = jnp.where(listed, 0.0, -FAR).astype(jnp.float32).transpose(0, 2, 1)
    bias = jnp.repeat(bias, TILE, axis=2)
    split = 2 if side_count == 2 else 1
    part = functools.partial(pool_part, bias=bias, scale=scale, head_size=head_size)

    if seq_count > 16:
        piece = share_halves(shared_keys, shared_values, "seq", quarter)
        step = seq_count // 2
        while step >= quarter:
            piece = share_step(piece, "seq", quarter, step)
            step //= 2
        shared = share_within(piece, "seq", quarter)
        everyone = jnp.arange(seq_count, dtype=jnp.int32)
        (sent,) = pack(send, everyone, keys, values, 0, [seq_count], bound, head_size)
        got = lax.all_to_all(sent, "seq", split_axis=0, concat_axis=0, tiled=True)
        tables = listing(everyone, everyone * bound)
        qt, *state = part(tables, queries, [got], state=None)
        state = shared_part(qt, shared, state, scale)
        tables = (*tables[:2], 0 * tables[2], tables[3])
        last = functools.partial(part, tables, qt, [got], state=state)
    else:
        order = [4, 8, 5, 9, 1, 2, 10, 3, 11, 6, 7, 12, 13, 14, 15, 0]
        partners = me ^ jnp.asarray(order, jnp.int32)
        where = {d: i for i, d in enumerate(order)}

        def use(state, blocks, ds, **kwargs):
            owners = jnp.stack([partners[where[d]] for d in ds])
            tables = listing(owners, bound * jnp.arange(len(ds)))
            q = queries if state is None else qt
            return part(tables, q, [blocks[d] for d in ds], state=state, **kwargs)

        def move(ds):
            return {
                d: lax.ppermute(parts[d], "seq", [(j, j ^ d) for j in range(seq_count)])
                for d in ds
            }

        def fence(*values):
            return lax.optimization_barrier(values)

        parts = {}
        for ds in ([4, 8, 5, 9], [1, 2, 10, 3, 11], [6, 12, 13, 14, 15, 0]):
            sizes = [2 if d == 6 else 1 for d in ds]
            lo = order.index(ds[0])
            parts.update(
                zip(ds, pack(send, partners, keys, values, lo, sizes, bound, head_size))
            )

        piece = share_halves(shared_keys, shared_values, "seq", quarter)
        first = [5, 1, 2, 10, 3, 11]
        got = move([4, 8, 5, 9])
        piece, parts[4] = fence(piece, parts[4])
        piece = share_step(piece, "seq", quarter, half_count)
        for d, earlier in ((1, 4), (10, 8), (2, 1), (11, 9), (3, 2)):
            parts[d], got[earlier] = fence(parts[d], got[earlier])
            got.update(move([d]))
        piece = share_step(piece, "seq", quarter, quarter)
        got[0] = parts[0]
        qt, *state = use(None, got, [0, 4, 8, 9])
        parts, got, piece, qt, state = fence(parts, got, piece, qt, state)

        shared = share_within(piece, "seq", quarter)
        new = move([6, 12, 13, 14, 15])
        state = use(state, got, first)
        state = use(state, new, [12])
        shared, *state = fence(shared, *state)
        state = shared_part(qt, shared, state, scale)
        both, *state = fence(new[6], *state)
        new[6], parts[1] = both[:bound], both[bound:]
        new[7] = move([1])[1]
        state = use(state, new, [6, 13])
        state = use(state, new, [7, 14])
        last = functools.partial(use, state, new, [15])

    if split == 1:
        (out,) = last(split=1)
        return lax.all_to_all(out, "head", split_axis=0, concat_axis=1, tiled=True)

    third = head_count // 3
    result = jnp.zeros((rows // 2, 2 * width), jnp.bfloat16)
    kept = []
    arrived = []
    for lo, hi in ((0, third), (third, 2 * third), (2 * third, head_count)):
        keep, away = last(split=2, heads=(lo, hi))
        kept.append((lo, keep))
        arrived.append((lo, lax.ppermute(away, "head", [(0, 1), (1, 0)])))
    for lo, block in kept:
        result = lax.dynamic_update_slice(result, block, (0, side * width + lo * head_size))
    for lo, block in arrived:
        result = lax.dynamic_update_slice(
            result, block, (0, (1 - side) * width + lo * head_size)
        )
    return result


def solution(mesh):
    return jax.shard_map(
        body,
        mesh=mesh,
        in_specs=(
            P("seq", "head"),
            P("seq", "head"),
            P("seq", "head"),
            P("head", None),
            P("head", "seq", None),
            P(),
        ),
        out_specs=P(("seq", "head"), None),
        check_vma=False,
    )
```

```python
import functools

import jax
import jax.numpy as jnp
from jax import lax
from jax.experimental import pallas as pl
from jax.experimental.pallas import tpu as pltpu
from jax.sharding import PartitionSpec as P

TILE = 128
SHARED = 4
FAR = 1e30
LOG2E = 1.4426950408889634
VMEM_BYTES = 56 * 1024 * 1024
WORK_BYTES = 12 * 1024 * 1024


def pack_kernel(lo, bound, head_size, codes_ref, order_ref, keys_ref, values_ref, *out_refs):
    at = lo
    for out_ref in out_refs:
        readers = out_ref.shape[0] // bound

        def one(i, _):
            code = codes_ref[order_ref[at + i // bound] * bound + i % bound]
            rows = pl.ds(pl.multiple_of(code % 65536 * TILE, TILE), TILE)
            cols = pl.ds(pl.multiple_of(code // 65536 * head_size, head_size), head_size)
            out_ref[i, 0] = keys_ref[rows, cols]
            out_ref[i, 1] = values_ref[rows, cols]
            return 0

        lax.fori_loop(0, readers * bound, one, 0)
        at += readers


def pack(codes, order, keys, values, lo, sizes, bound, head_size):
    shapes = [
        jax.ShapeDtypeStruct((n * bound, 2, TILE, head_size), keys.dtype) for n in sizes
    ]
    whole = pl.BlockSpec(keys.shape, lambda i, *_: (0, 0))
    return pl.pallas_call(
        functools.partial(pack_kernel, lo, bound, head_size),
        grid_spec=pltpu.PrefetchScalarGridSpec(
            num_scalar_prefetch=2,
            grid=(1,),
            in_specs=[whole, whole],
            out_specs=[pl.BlockSpec(t.shape, lambda i, *_: (0, 0, 0, 0)) for t in shapes],
        ),
        out_shape=shapes,
        compiler_params=pltpu.CompilerParams(vmem_limit_bytes=VMEM_BYTES),
        name="pack_tiles",
    )(codes, order, keys, values)


def absorb(scale, block, k, vt, bias_row, qt_ref, acc_ref, m_ref, l_ref):
    for start in range(0, qt_ref.shape[2], block):
        cols = slice(start, start + block)
        s = jnp.dot(k, qt_ref[0, :, cols], preferred_element_type=jnp.float32)
        top = jnp.max(s, 0, keepdims=True) * scale
        m_old = m_ref[0, :, cols]
        if bias_row is None:
            m_new = jnp.maximum(m_old, top)
            shift = m_new
        else:
            bias = bias_row[:, cols]
            m_new = jnp.maximum(m_old, top + bias)
            shift = m_new - bias
        alpha = jnp.exp2(m_old - m_new)
        p = jnp.exp2(s * scale - shift)
        m_ref[0, :, cols] = m_new
        l_ref[0, :, cols] = l_ref[0, :, cols] * alpha + jnp.sum(p, 0, keepdims=True)
        acc_ref[0, :, cols] = acc_ref[0, :, cols] * alpha + jnp.dot(
            vt, p.astype(jnp.bfloat16), preferred_element_type=jnp.float32
        )


def shared_kernel(scale, block, qt_ref, k_ref, v_ref, acc_in, m_in, l_in, acc_ref, m_ref, l_ref):
    acc_ref[...] = acc_in[...]
    m_ref[...] = m_in[...]
    l_ref[...] = l_in[...]
    for j in range(SHARED):
        rows = slice(j * TILE, (j + 1) * TILE)
        absorb(
            scale, block, k_ref[rows, :], v_ref[rows, :].T, None, qt_ref, acc_ref, m_ref, l_ref
        )


def shared_part(qt, shared, state, scale):
    head_count, head_size, rows = qt.shape
    stat_spec = pl.BlockSpec((1, 1, rows), lambda h: (h, 0, 0))
    wide_spec = pl.BlockSpec((1, head_size, rows), lambda h: (h, 0, 0))
    keys = SHARED * TILE
    return pl.pallas_call(
        functools.partial(shared_kernel, scale, min(256, rows)),
        grid=(head_count,),
        out_shape=[jax.ShapeDtypeStruct(a.shape, a.dtype) for a in state],
        in_specs=[
            wide_spec,
            pl.BlockSpec((keys, head_size), lambda h: (0, h)),
            pl.BlockSpec((keys, head_size), lambda h: (2, h)),
            wide_spec,
            stat_spec,
            stat_spec,
        ],
        out_specs=[wide_spec, stat_spec, stat_spec],
        compiler_params=pltpu.CompilerParams(vmem_limit_bytes=WORK_BYTES),
        name="shared_tiles",
    )(qt, shared, shared, *state)


def pool_kernel(
    scale, block, parts, first, split, head_lo,
    place_ref, entry_ref, count_ref, side_ref, q_ref, bias_ref, *refs,
):
    tiles = refs[:parts]
    held_ref, sems = refs[-2:]
    refs = refs[parts:-2]
    head = pl.program_id(0) + head_lo
    copies = []
    at = 0
    for k, tiles_ref in enumerate(tiles):
        span = pl.ds(at, tiles_ref.shape[0])
        copies.append(pltpu.make_async_copy(tiles_ref, held_ref.at[span], sems.at[k]))
        at += tiles_ref.shape[0]

    @pl.when(pl.program_id(0) == 0)
    def _():
        for copy in copies:
            copy.start()

    if first:
        qt_ref, acc_ref, m_ref, l_ref = refs
        qt_ref[0] = q_ref[...].T
        acc_ref[...] = jnp.zeros_like(acc_ref)
        m_ref[...] = jnp.full_like(m_ref, -0.5 * FAR)
        l_ref[...] = jnp.zeros_like(l_ref)
    else:
        qt_ref = q_ref
        acc_in, m_in, l_in = refs[:3]
        acc_ref, m_ref, l_ref = refs[-3:]
        acc_ref[...] = acc_in[...]
        m_ref[...] = m_in[...]
        l_ref[...] = l_in[...]

    @pl.when(pl.program_id(0) == 0)
    def _():
        for copy in copies:
            copy.wait()

    def one(i):
        place = place_ref[head, i]
        entry = entry_ref[head, i]
        absorb(
            scale, block, held_ref[place, 0], held_ref[place, 1].T,
            bias_ref[0, pl.ds(entry, 1), :], qt_ref, acc_ref, m_ref, l_ref,
        )

    def two(i, _):
        one(2 * i)
        one(2 * i + 1)
        return 0

    total = count_ref[head]
    lax.fori_loop(0, total // 2, two, 0)

    @pl.when(total % 2 == 1)
    def _():
        one(total - 1)

    if split:
        out_refs, whole = refs[3:-4], refs[-4]
        rows = qt_ref.shape[2]
        for start in range(0, rows, block):
            cols = slice(start, start + block)
            out = (acc_ref[0, :, cols] * (1.0 / l_ref[0, :, cols])).astype(jnp.bfloat16)
            whole[cols, :] = out.T
        if split == 1:
            out_refs[0][...] = whole[...]
        else:
            half = rows // split
            for ref, side in zip(out_refs, (side_ref[0], 1 - side_ref[0])):
                ref[...] = whole[pl.ds(pl.multiple_of(side * half, half), half), :]


def pool_part(tables, q, tiles, bias, state, scale, head_size, split=0, heads=None):
    first = state is None
    head_count, pool_len, rows = bias.shape
    lo, hi = heads or (0, head_count)
    count = hi - lo
    stat_spec = pl.BlockSpec((1, 1, rows), lambda h, *_: (h + lo, 0, 0))
    wide_spec = pl.BlockSpec((1, head_size, rows), lambda h, *_: (h + lo, 0, 0))
    acc = jax.ShapeDtypeStruct((head_count, head_size, rows), jnp.float32)
    stat = jax.ShapeDtypeStruct((head_count, 1, rows), jnp.float32)
    q_spec = pl.BlockSpec((rows, head_size), lambda h, *_: (0, h)) if first else wide_spec
    in_specs = [q_spec, pl.BlockSpec((1, pool_len, rows), lambda h, *_: (h + lo, 0, 0))]
    in_specs += [pl.BlockSpec(memory_space=pl.ANY)] * len(tiles)
    if not first:
        in_specs += [wide_spec, stat_spec, stat_spec]
    scratch = []
    if split:
        out_rows = rows // split
        out_shape = [
            jax.ShapeDtypeStruct((out_rows, count * head_size), jnp.bfloat16)
        ] * split
        out_specs = [pl.BlockSpec((out_rows, head_size), lambda h, *_: (0, h))] * split
        scratch = [
            pltpu.VMEM((rows, head_size), jnp.bfloat16),
            pltpu.VMEM((1, head_size, rows), jnp.float32),
            pltpu.VMEM((1, 1, rows), jnp.float32),
            pltpu.VMEM((1, 1, rows), jnp.float32),
        ]
    else:
        out_shape = [acc, stat, stat]
        out_specs = [wide_spec, stat_spec, stat_spec]
        if first:
            out_shape = [jax.ShapeDtypeStruct(acc.shape, jnp.bfloat16)] + out_shape
            out_specs = [wide_spec] + out_specs
    places = sum(t.shape[0] for t in tiles)
    scratch += [
        pltpu.VMEM((places, 2, TILE, head_size), jnp.bfloat16),
        pltpu.SemaphoreType.DMA((len(tiles),)),
    ]
    return pl.pallas_call(
        functools.partial(pool_kernel, scale, min(256, rows), len(tiles), first, split, lo),
        grid_spec=pltpu.PrefetchScalarGridSpec(
            num_scalar_prefetch=4,
            grid=(count,),
            in_specs=in_specs,
            out_specs=out_specs,
            scratch_shapes=scratch,
        ),
        out_shape=out_shape,
        compiler_params=pltpu.CompilerParams(
            vmem_limit_bytes=WORK_BYTES + places * 2 * TILE * head_size * 2
        ),
        name="pool_tiles",
    )(*tables, q, bias, *tiles, *(() if first else state))


def share_halves(keys, values, axis, size):
    me = lax.axis_index(axis)
    got = lax.ppermute(values, axis, [(0, size // 2)])
    return jnp.where(me % size == size // 2, got, keys)


def share_step(piece, axis, size, step):
    count = lax.axis_size(axis)
    me = lax.axis_index(axis)
    pairs = [
        (j + k, j + k + step) for j in range(0, count, 2 * step) for k in (0, size // 2)
    ]
    over = lax.ppermute(piece, axis, pairs)
    return jnp.where(me // step % 2 == 1, over, piece)


def share_within(piece, axis, size):
    groups = [list(range(i, i + size)) for i in range(0, lax.axis_size(axis), size)]
    return lax.all_gather(piece, axis, axis=0, tiled=True, axis_index_groups=groups)


def body(queries, keys, values, tile_pool, tile_lists, key_slot):
    seq_count = lax.axis_size("seq")
    side_count = lax.axis_size("head")
    me = lax.axis_index("seq")
    side = lax.axis_index("head")
    head_count, pool_total = tile_pool.shape
    pool_len = pool_total // seq_count
    rows, width = queries.shape
    head_size = width // head_count
    tile_count = rows // TILE
    bound = (head_count * pool_len + seq_count - 1) // seq_count
    scale = head_size ** (-0.5) * LOG2E
    entries = head_count * pool_len

    shared_keys, shared_values = keys[: SHARED * TILE], values[: SHARED * TILE]
    quarter = 4

    tiles_all = jnp.arange(key_slot.shape[0], dtype=jnp.int32)
    storage = jnp.sum(
        jnp.where(tile_pool[:, :, None] == tiles_all, key_slot, 0), -1
    ).reshape(head_count, seq_count, pool_len)
    by_reader = storage.transpose(1, 0, 2).reshape(seq_count, entries)
    ids = jnp.arange(entries, dtype=jnp.int32)
    before = (ids[:, None] < ids[None, :]).astype(jnp.bfloat16)
    wanted = by_reader // tile_count == me
    place = jnp.dot(
        wanted.astype(jnp.bfloat16), before, preferred_element_type=jnp.float32
    ).astype(jnp.int32)
    place = jnp.where(wanted, place, -1)
    code = (ids // pool_len)[None, :] * 65536 + by_reader % tile_count
    slots = jnp.arange(bound, dtype=jnp.int32)
    send = jnp.sum(
        jnp.where(place[:, None, :] == slots[None, :, None], code[:, None, :], 0), -1
    ).reshape(-1)

    own = lax.dynamic_index_in_dim(by_reader, me, 0, keepdims=False)
    owner = own // tile_count
    same = (owner[:, None] == owner[None, :]) & (ids[:, None] < ids[None, :])
    position = jnp.sum(same.astype(jnp.int32), 0).reshape(head_count, pool_len)
    owner = owner.reshape(head_count, pool_len)
    pool_ids = jnp.arange(pool_len, dtype=jnp.int32)

    def listing(owners, bases):
        match = owner[:, :, None] == owners
        here = jnp.any(match, -1)
        base = jnp.sum(jnp.where(match, bases, 0), -1)
        rank = jnp.sum(
            (here[:, :, None] & (pool_ids[:, None] < pool_ids[None, :])).astype(jnp.int32), 1
        )
        rank = jnp.where(here, rank, -1)
        hit = rank[:, None, :] == pool_ids[None, :, None]
        entry = jnp.sum(jnp.where(hit, pool_ids, 0), -1)
        place = base + position
        place = jnp.sum(jnp.where(hit, place[:, None, :], 0), -1)
        return place, entry, jnp.sum(here.astype(jnp.int32), 1), side.reshape(1)

    half_count = seq_count // 2
    listed = jnp.any(
        tile_lists[:, :, :, None] == jnp.arange(pool_len, dtype=jnp.int32), 2
    )
    bias = jnp.where(listed, 0.0, -FAR).astype(jnp.float32).transpose(0, 2, 1)
    bias = jnp.repeat(bias, TILE, axis=2)
    split = 2 if side_count == 2 else 1
    part = functools.partial(pool_part, bias=bias, scale=scale, head_size=head_size)

    if seq_count > 16:
        piece = share_halves(shared_keys, shared_values, "seq", quarter)
        step = seq_count // 2
        while step >= quarter:
            piece = share_step(piece, "seq", quarter, step)
            step //= 2
        shared = share_within(piece, "seq", quarter)
        everyone = jnp.arange(seq_count, dtype=jnp.int32)
        (sent,) = pack(send, everyone, keys, values, 0, [seq_count], bound, head_size)
        got = lax.all_to_all(sent, "seq", split_axis=0, concat_axis=0, tiled=True)
        tables = listing(everyone, everyone * bound)
        qt, *state = part(tables, queries, [got], state=None)
        state = shared_part(qt, shared, state, scale)
        tables = (*tables[:2], 0 * tables[2], tables[3])
        last = functools.partial(part, tables, qt, [got], state=state)
    else:
        order = [4, 8, 5, 9, 1, 2, 10, 3, 11, 6, 7, 12, 13, 14, 15, 0]
        partners = me ^ jnp.asarray(order, jnp.int32)
        where = {d: i for i, d in enumerate(order)}

        def use(state, blocks, ds, **kwargs):
            owners = jnp.stack([partners[where[d]] for d in ds])
            tables = listing(owners, bound * jnp.arange(len(ds)))
            q = queries if state is None else qt
            return part(tables, q, [blocks[d] for d in ds], state=state, **kwargs)

        def move(ds):
            return {
                d: lax.ppermute(parts[d], "seq", [(j, j ^ d) for j in range(seq_count)])
                for d in ds
            }

        def fence(*values):
            return lax.optimization_barrier(values)

        parts = {}
        for ds in ([4, 8, 5, 9], [1, 2, 10, 3, 11], [6, 12, 13, 14, 15, 0]):
            sizes = [2 if d == 6 else 1 for d in ds]
            lo = order.index(ds[0])
            parts.update(
                zip(ds, pack(send, partners, keys, values, lo, sizes, bound, head_size))
            )

        piece = share_halves(shared_keys, shared_values, "seq", quarter)
        first = [5, 1, 2, 10, 3, 11]
        got = move([4, 8, 5, 9])
        piece, parts[4] = fence(piece, parts[4])
        piece = share_step(piece, "seq", quarter, half_count)
        for d, earlier in ((1, 4), (10, 8), (2, 1), (11, 9), (3, 2)):
            parts[d], got[earlier] = fence(parts[d], got[earlier])
            got.update(move([d]))
        piece = share_step(piece, "seq", quarter, quarter)
        got[0] = parts[0]
        qt, *state = use(None, got, [0, 4, 8, 9])
        parts, got, piece, qt, state = fence(parts, got, piece, qt, state)

        shared = share_within(piece, "seq", quarter)
        new = move([6, 12, 13, 14, 15])
        state = use(state, got, first)
        state = use(state, new, [12])
        shared, *state = fence(shared, *state)
        state = shared_part(qt, shared, state, scale)
        both, *state = fence(new[6], *state)
        new[6], parts[1] = both[:bound], both[bound:]
        new[7] = move([1])[1]
        state = use(state, new, [6, 13])
        state = use(state, new, [7, 14])
        last = functools.partial(use, state, new, [15])

    if split == 1:
        (out,) = last(split=1)
        return lax.all_to_all(out, "head", split_axis=0, concat_axis=1, tiled=True)

    fourth = head_count // 4
    result = jnp.zeros((rows // 2, 2 * width), jnp.bfloat16)
    kept = []
    arrived = []
    for lo in range(0, head_count, fourth):
        hi = lo + fourth
        keep, away = last(split=2, heads=(lo, hi))
        kept.append((lo, keep))
        arrived.append((lo, lax.ppermute(away, "head", [(0, 1), (1, 0)])))
    for lo, block in kept:
        result = lax.dynamic_update_slice(result, block, (0, side * width + lo * head_size))
    for lo, block in arrived:
        result = lax.dynamic_update_slice(
            result, block, (0, (1 - side) * width + lo * head_size)
        )
    return result


def solution(mesh):
    return jax.shard_map(
        body,
        mesh=mesh,
        in_specs=(
            P("seq", "head"),
            P("seq", "head"),
            P("seq", "head"),
            P("head", None),
            P("head", "seq", None),
            P(),
        ),
        out_specs=P(("seq", "head"), None),
        check_vma=False,
    )
```
